32 devices in a mesh: group: 2 (over y), sample: 8 (over z, x), mode: 2 (over core).
Axes of the slice: x: 2, y: 2, z: 4, core: 2. Of those that a mesh axis runs over, the one named last changes fastest.
Arguments:
- displace: bfloat16 [8192, 3072], P(('group', 'sample')), parts along dimension 0, may hold values from -6 to 6
- forces: bfloat16 [8192, 3072], P(('group', 'sample'), 'mode'), parts along dimension 0, may hold values from -6 to 6
- trial: bfloat16 [6144, 512], P(('group', 'sample'), 'mode'), parts along dimension 0, may hold values from -0.109375 to 0.109375
Outputs:
- hess_block: float32 [6144, 512], P(('group', 'sample'), 'mode'), parts along dimension 0
The draws below stay inside these ranges and needn't reach their ends.
There are 2 independent parts, one for each index of `group`. The reference program is written for one: setup_inputs(seed, part) draws one part's arguments, and reference() takes and returns one part's arrays. A program takes and returns all parts, laid end to end along the dimension named above; each array names one. Nothing has to cross between parts.
All inputs are finite; a program needn't handle non-finite values.
Results may differ from the reference program's by a relative error of at most 0.0028.
Values may be sent and summed in bfloat16 or wider, within the bound.
A program may use at most 64 MiB of HBM per device.

```python
import math
import jax
import jax.numpy as jnp
from jax import lax

M = 3072
K = 512
SAMPLES = 4096


def raised(entries, own_key, source, target, blocks, factor):
    def block_of(dim):
        return (jnp.arange(entries.shape[dim]) // (entries.shape[dim] // blocks)).reshape((-1,) + (1,) * (entries.ndim - 1 - dim))

    one_side = jax.random.permutation(own_key, blocks)[block_of(target)]
    far = (block_of(target) + blocks // 2) % blocks
    return jnp.where((block_of(source) == one_side) | (block_of(source) == far), factor * entries, entries)


def levels(key, shape, pieces, least, largest):
    level = 1.0
    for axis_at, shards_of in pieces:
        draws = jax.random.uniform(jax.random.fold_in(jax.random.fold_in(key, 6), axis_at), (shards_of,), jnp.float32, least / len(pieces), largest / len(pieces))
        level = level * jnp.repeat(jnp.exp(draws), shape[axis_at] // shards_of).reshape((-1,) + (1,) * (len(shape) - 1 - axis_at))
    return level


def gaussian(rng, dims, spread, reach, cuts=(), held_as=jnp.bfloat16):
    loudness = levels(rng, dims, cuts, -0.22, 0.18) if cuts else 1.0
    array = jax.random.normal(rng, dims, jnp.float32) * spread * loudness
    return jnp.minimum(jnp.maximum(array, -reach), reach).astype(held_as)


def gaussian_with(own_key, shape, spread, bound, pieces, heavy, dtype=jnp.bfloat16):
    values = spread * jax.random.normal(own_key, shape, jnp.float32)
    if pieces:
        values = values * levels(own_key, shape, pieces, -0.22, 0.18)
    return jnp.clip(raised(values, jax.random.fold_in(own_key, 3), *heavy), -bound, bound).astype(dtype)


def setup_inputs(seed: int = 0, part: int = 0) -> dict:
    key_list = jax.random.split(jax.random.key(seed), 4)
    part_splits = jax.random.split(jax.random.fold_in(key_list[3], part), 4)
    displace = gaussian_with(part_splits[0], (SAMPLES, M), 1.0, 6.0, ((0, 8),), (0, 1, 8, 2.0))
    forces = gaussian(part_splits[1], (SAMPLES, M), 1.0, 6.0, ((0, 8), (1, 2)))
    trial = gaussian(part_splits[2], (M, K), M ** -0.5, 0.109375, ((0, 8), (1, 2)))
    return dict(displace=displace, forces=forces, trial=trial)


def reference(displace, forces, trial):
    proj_x = jnp.dot(displace, trial, preferred_element_type=jnp.float32)
    proj_f = jnp.dot(forces, trial, preferred_element_type=jnp.float32)
    weights = lax.optimization_barrier(jnp.sum(displace.astype(jnp.float32) * forces.astype(jnp.float32), axis=1)) / math.sqrt(M)
    scaled_x = (weights[:, None] * proj_x).astype(jnp.bfloat16)
    scaled_f = (weights[:, None] * proj_f).astype(jnp.bfloat16)
    left = jnp.dot(displace.T, scaled_f, preferred_element_type=jnp.float32)
    right = jnp.dot(forces.T, scaled_x, preferred_element_type=jnp.float32)
    return (left + right) / (2.0 * math.sqrt(SAMPLES))
```

```python
import functools
import math

import jax
import jax.numpy as jnp
from jax import lax
from jax.experimental import pallas as pl
from jax.experimental.pallas import tpu as pltpu
from jax.sharding import PartitionSpec as P

MESH = pl.DeviceIdType.MESH
PAIR = 2
LANES = 128


def contract_rows(columns, scaled):
    return lax.dot_general(
        columns, scaled, (((0,), (0,)), ((), ())), preferred_element_type=jnp.float32
    )


def plain_shards(displace, forces, trial):
    full_forces = lax.all_gather(forces, "mode", axis=1, tiled=True)
    modes_all = displace.shape[1]
    own_modes = forces.shape[1]
    own_disp = lax.dynamic_slice_in_dim(displace, lax.axis_index("mode") * own_modes, own_modes, 1)
    partial_value = jnp.sum(own_disp.astype(jnp.float32) * forces.astype(jnp.float32), axis=1)
    weights = lax.psum(partial_value, "mode") / math.sqrt(modes_all)
    piece = lax.all_gather(trial, "sample", axis=0, tiled=True)
    proj_x = jnp.dot(displace, piece, preferred_element_type=jnp.float32)
    proj_f = jnp.dot(full_forces, piece, preferred_element_type=jnp.float32)
    scaled_x = (weights[:, None] * proj_x).astype(jnp.bfloat16)
    scaled_f = (weights[:, None] * proj_f).astype(jnp.bfloat16)
    samples_all = displace.shape[0] * lax.axis_size("sample")
    result = lax.psum_scatter(
        contract_rows(displace, scaled_f) + contract_rows(full_forces, scaled_x),
        "sample",
        scatter_dimension=0,
        tiled=True,
    )
    return result / (2.0 * math.sqrt(samples_all))


def kernel(n, displace_ref, forces_ref, trial_ref, out_ref, dv, fv, dt, ft, tb, px, pf, wacc, sx, sf,
           xsend, xrecv, zsend, zrecv, own_sum, local_sem, mode_sem, gather_recv, line_send, pair_send,
           xs_sem, xr_sem, zs_sem, zr_sem):
    line = n // PAIR
    g, s, c = lax.axis_index("group"), lax.axis_index("sample"), lax.axis_index("mode")
    z, x = s // PAIR, s % PAIR
    other = 1 - x
    rows = trial_ref.shape[0]
    modes = displace_ref.shape[1]
    own_modes = forces_ref.shape[1]

    def at(zz, xx):
        return (g, zz * PAIR + xx, c)

    def cols(owner):
        return pl.ds(pl.multiple_of(owner * rows, LANES), rows)

    half = pl.ds(pl.multiple_of(c * own_modes, LANES), own_modes)
    load_t = pltpu.make_async_copy(trial_ref, tb.at[s], local_sem.at[0])
    load_f = pltpu.make_async_copy(forces_ref, fv.at[:, half], local_sem.at[1])
    load_d = pltpu.make_async_copy(displace_ref, dv, local_sem.at[2])
    load_t.start()
    load_f.start()
    load_d.start()

    barrier = pltpu.get_barrier_semaphore()
    pl.semaphore_signal(barrier, inc=1, device_id=(g, s, 1 - c), device_id_type=MESH)
    pl.semaphore_signal(barrier, inc=1, device_id=at(z, other), device_id_type=MESH)

    def greet(j, carry):
        pl.semaphore_signal(
            barrier, inc=1, device_id=at(lax.rem(z + 1 + j, line), x), device_id_type=MESH
        )
        return carry

    lax.fori_loop(0, line - 1, greet, 0)
    pl.semaphore_wait(barrier, line + 1)

    def line_copy(d, zl):
        sgn = 2 * d - 1
        owner = zl * PAIR + x
        return pltpu.make_async_remote_copy(
            src_ref=tb.at[owner], dst_ref=tb.at[owner], send_sem=line_send.at[d, zl],
            recv_sem=gather_recv.at[owner], device_id=at(z - sgn, x), device_id_type=MESH,
        )

    def pair_copy(zl):
        owner = zl * PAIR + x
        return pltpu.make_async_remote_copy(
            src_ref=tb.at[owner], dst_ref=tb.at[owner], send_sem=pair_send.at[zl],
            recv_sem=gather_recv.at[owner], device_id=at(z, other), device_id_type=MESH,
        )

    def arrived(owner):
        pltpu.make_async_remote_copy(
            src_ref=tb.at[owner], dst_ref=tb.at[owner], send_sem=pair_send.at[0],
            recv_sem=gather_recv.at[owner], device_id=at(z, other), device_id_type=MESH,
        ).wait_recv()

    def inside(zz):
        return jnp.logical_and(zz >= 0, zz < line)

    load_t.wait()
    for d in (0, 1):
        @pl.when(inside(z - (2 * d - 1)))
        def _():
            line_copy(d, z).start()
    pair_copy(z).start()

    load_f.wait()
    swap = pltpu.make_async_remote_copy(
        src_ref=fv.at[:, half], dst_ref=fv.at[:, half], send_sem=mode_sem.at[0],
        recv_sem=mode_sem.at[1], device_id=(g, s, 1 - c), device_id_type=MESH,
    )
    swap.start()
    px[...] = jnp.zeros_like(px)
    pf[...] = jnp.zeros_like(pf)
    wacc[...] = jnp.zeros_like(wacc)
    load_d.wait()
    other_half = pl.ds(pl.multiple_of((1 - c) * own_modes, LANES), own_modes)
    pltpu.make_async_remote_copy(
        src_ref=fv.at[:, other_half], dst_ref=fv.at[:, other_half], send_sem=mode_sem.at[0],
        recv_sem=mode_sem.at[1], device_id=(g, s, 1 - c), device_id_type=MESH,
    ).wait_recv()

    def prepare(owner):
        d_cols = dv[:, cols(owner)]
        f_cols = fv[:, cols(owner)]
        dt[owner] = d_cols.T
        ft[owner] = f_cols.T
        product = d_cols.astype(jnp.float32) * f_cols.astype(jnp.float32)
        total = product[:, :LANES]
        for b in range(1, rows // LANES):
            total += product[:, b * LANES:(b + 1) * LANES]
        wacc[...] += total

    def project(owner):
        block = tb[owner]
        px[...] += jnp.dot(dv[:, cols(owner)], block, preferred_element_type=jnp.float32)
        pf[...] += jnp.dot(fv[:, cols(owner)], block, preferred_element_type=jnp.float32)

    project(s)

    def gather_step(t, carry):
        for d in (0, 1):
            sgn = 2 * d - 1
            zl = z + sgn * t

            @pl.when(jnp.logical_and(inside(zl), t > 0))
            def _():
                arrived(zl * PAIR + x)

                @pl.when(inside(z - sgn))
                def _():
                    line_copy(d, zl).start()

                pair_copy(zl).start()

        @pl.when(t < line)
        def _():
            for k in range(PAIR):
                prepare(t * PAIR + k)

        for d in (0, 1):
            sgn = 2 * d - 1
            zl = z + sgn * t

            @pl.when(jnp.logical_and(inside(zl), t > 0))
            def _():
                project(zl * PAIR + x)

            u = t - 1
            zu = z + sgn * u

            @pl.when(jnp.logical_and(inside(zu), jnp.logical_or(u > 0, u + 1 - d == 1)))
            def _():
                arrived(zu * PAIR + other)
                project(zu * PAIR + other)

        return carry

    lax.fori_loop(0, line + 1, gather_step, 0)

    weights = jnp.sum(wacc[...], axis=1, keepdims=True) / math.sqrt(modes)
    sx[...] = (weights * px[...]).astype(jnp.bfloat16)
    sf[...] = (weights * pf[...]).astype(jnp.bfloat16)

    def term(owner):
        return jnp.dot(dt[owner], sf[...], preferred_element_type=jnp.float32) + jnp.dot(
            ft[owner], sx[...], preferred_element_type=jnp.float32
        )

    def x_copy(j):
        return pltpu.make_async_remote_copy(
            src_ref=xsend.at[j], dst_ref=xrecv.at[j], send_sem=xs_sem.at[j],
            recv_sem=xr_sem.at[j], device_id=at(z, other), device_id_type=MESH,
        )

    def z_copy(j):
        return pltpu.make_async_remote_copy(
            src_ref=zsend.at[j], dst_ref=zrecv.at[j], send_sem=zs_sem.at[j],
            recv_sem=zr_sem.at[j], device_id=at(lax.rem(z + 1 + j, line), x), device_id_type=MESH,
        )

    def send_pair(j, carry):
        xsend[j] = term(lax.rem(z + 1 + j, line) * PAIR + other).astype(jnp.bfloat16)
        x_copy(j).start()
        return carry

    lax.fori_loop(0, line, send_pair, 0)

    def send_line(j, carry):
        own_sum[...] = term(lax.rem(z + 1 + j, line) * PAIR + x)
        x_copy(j).wait_recv()

        @pl.when(j < line - 1)
        def _():
            zsend[j] = (own_sum[...] + xrecv[j].astype(jnp.float32)).astype(jnp.bfloat16)
            z_copy(j).start()

        @pl.when(j == line - 1)
        def _():
            out_ref[...] = own_sum[...] + xrecv[j].astype(jnp.float32)

        return carry

    lax.fori_loop(0, line, send_line, 0)

    swap.wait_send()

    def drain(zl, carry):
        pair_copy(zl).wait_send()
        for d in (0, 1):
            sgn = 2 * d - 1
            came = (zl - z) * sgn >= 0

            @pl.when(jnp.logical_and(came, inside(z - sgn)))
            def _():
                line_copy(d, zl).wait_send()

        x_copy(zl).wait_send()
        return carry

    lax.fori_loop(0, line, drain, 0)

    def finish(j, carry):
        z_copy(j).wait_recv()
        out_ref[...] += zrecv[j].astype(jnp.float32)
        z_copy(j).wait_send()
        return carry

    lax.fori_loop(0, line - 1, finish, 0)
    out_ref[...] = out_ref[...] / (2.0 * math.sqrt(displace_ref.shape[0] * n))


def kernel_shards(displace, forces, trial):
    n = lax.axis_size("sample")
    line = n // PAIR
    samples, modes = displace.shape
    rows, width = trial.shape
    bf, f32 = jnp.bfloat16, jnp.float32
    dma = pltpu.SemaphoreType.DMA
    any_spec = pl.BlockSpec(memory_space=pl.ANY)
    return pl.pallas_call(
        functools.partial(kernel, n),
        out_shape=jax.ShapeDtypeStruct((rows, width), f32),
        in_specs=[any_spec] * 3,
        out_specs=pl.BlockSpec(memory_space=pltpu.VMEM),
        scratch_shapes=[
            pltpu.VMEM((samples, modes), bf),
            pltpu.VMEM((samples, modes), bf),
            pltpu.VMEM((n, rows, samples), bf),
            pltpu.VMEM((n, rows, samples), bf),
            pltpu.VMEM((n, rows, width), bf),
            pltpu.VMEM((samples, width), f32),
            pltpu.VMEM((samples, width), f32),
            pltpu.VMEM((samples, LANES), f32),
            pltpu.VMEM((samples, width), bf),
            pltpu.VMEM((samples, width), bf),
            pltpu.VMEM((line, rows, width), bf),
            pltpu.VMEM((line, rows, width), bf),
            pltpu.VMEM((line, rows, width), bf),
            pltpu.VMEM((line, rows, width), bf),
            pltpu.VMEM((rows, width), f32),
            dma((3,)),
            dma((2,)),
            dma((n,)),
            dma((2, line)),
            dma((line,)),
            dma((line,)),
            dma((line,)),
            dma((line,)),
            dma((line,)),
        ],
        compiler_params=pltpu.CompilerParams(
            collective_id=0, has_side_effects=True, vmem_limit_bytes=48 * 1024 * 1024
        ),
        cost_estimate=pl.CostEstimate(
            flops=8 * samples * modes * width, bytes_accessed=4 * samples * modes, transcendentals=0
        ),
    )(displace, forces, trial)


def fits(displace, forces, trial):
    n = lax.axis_size("sample")
    rows, width = trial.shape
    samples = displace.shape[0]
    aligned = all(size % LANES == 0 for size in (rows, width, samples, forces.shape[1]))
    return aligned and n % PAIR == 0 and n > PAIR and lax.axis_size("mode") == 2


def shards(displace, forces, trial):
    if fits(displace, forces, trial):
        return kernel_shards(displace, forces, trial)
    return plain_shards(displace, forces, trial)


def solution(mesh):
    return jax.shard_map(
        shards,
        mesh=mesh,
        in_specs=(
            P(("group", "sample"), None),
            P(("group", "sample"), "mode"),
            P(("group", "sample"), "mode"),
        ),
        out_specs=P(("group", "sample"), "mode"),
        check_vma=False,
    )
```

```python
import functools
import math

import jax
import jax.numpy as jnp
from jax import lax
from jax.experimental import pallas as pl
from jax.experimental.pallas import tpu as pltpu
from jax.sharding import PartitionSpec as P

MESH = pl.DeviceIdType.MESH
PAIR = 2
LANES = 128
HALVES = 2


def contract_rows(columns, scaled):
    return lax.dot_general(
        columns, scaled, (((0,), (0,)), ((), ())), preferred_element_type=jnp.float32
    )


def plain_shards(displace, forces, trial):
    full_forces = lax.all_gather(forces, "mode", axis=1, tiled=True)
    modes_all = displace.shape[1]
    own_modes = forces.shape[1]
    own_disp = lax.dynamic_slice_in_dim(displace, lax.axis_index("mode") * own_modes, own_modes, 1)
    partial_value = jnp.sum(own_disp.astype(jnp.float32) * forces.astype(jnp.float32), axis=1)
    weights = lax.psum(partial_value, "mode") / math.sqrt(modes_all)
    piece = lax.all_gather(trial, "sample", axis=0, tiled=True)
    proj_x = jnp.dot(displace, piece, preferred_element_type=jnp.float32)
    proj_f = jnp.dot(full_forces, piece, preferred_element_type=jnp.float32)
    scaled_x = (weights[:, None] * proj_x).astype(jnp.bfloat16)
    scaled_f = (weights[:, None] * proj_f).astype(jnp.bfloat16)
    samples_all = displace.shape[0] * lax.axis_size("sample")
    result = lax.psum_scatter(
        contract_rows(displace, scaled_f) + contract_rows(full_forces, scaled_x),
        "sample",
        scatter_dimension=0,
        tiled=True,
    )
    return result / (2.0 * math.sqrt(samples_all))


def kernel(n, displace_ref, forces_ref, trial_ref, out_ref, dv, fv, dt, ft, tb, px, pf, wacc, sx, sf,
           xsend, xrecv, zsend, zrecv, own_sum, local_sem, mode_sem, gather_recv, line_send, pair_send,
           xs_sem, xr_sem, zs_sem, zr_sem):
    line = n // PAIR
    g, s, c = lax.axis_index("group"), lax.axis_index("sample"), lax.axis_index("mode")
    z, x = s // PAIR, s % PAIR
    other = 1 - x
    rows = trial_ref.shape[0]
    modes = displace_ref.shape[1]
    own_modes = forces_ref.shape[1]
    piece = rows // HALVES

    def at(zz, xx):
        return (g, zz * PAIR + xx, c)

    def cols(owner):
        return pl.ds(pl.multiple_of(owner * rows, LANES), rows)

    half = pl.ds(pl.multiple_of(c * own_modes, LANES), own_modes)
    load_t = pltpu.make_async_copy(trial_ref, tb.at[s], local_sem.at[0])
    load_f = pltpu.make_async_copy(forces_ref, fv.at[:, half], local_sem.at[1])
    load_d = pltpu.make_async_copy(displace_ref, dv, local_sem.at[2])
    load_t.start()
    load_f.start()
    load_d.start()

    barrier = pltpu.get_barrier_semaphore()
    pl.semaphore_signal(barrier, inc=1, device_id=(g, s, 1 - c), device_id_type=MESH)
    pl.semaphore_signal(barrier, inc=1, device_id=at(z, other), device_id_type=MESH)

    def greet(j, carry):
        pl.semaphore_signal(
            barrier, inc=1, device_id=at(lax.rem(z + 1 + j, line), x), device_id_type=MESH
        )
        return carry

    lax.fori_loop(0, line - 1, greet, 0)
    pl.semaphore_wait(barrier, line + 1)

    def tile(h):
        return pl.ds(pl.multiple_of(h * piece, piece), piece)

    def shard_copy(owner, h, send_sem, target):
        part = tb.at[owner, tile(h)]
        return pltpu.make_async_remote_copy(
            src_ref=part, dst_ref=part, send_sem=send_sem,
            recv_sem=gather_recv.at[owner, h], device_id=target, device_id_type=MESH,
        )

    def line_copy(d, zl, h):
        sgn = 2 * d - 1
        return shard_copy(zl * PAIR + x, h, line_send.at[d, zl, h], at(z - sgn, x))

    def pair_copy(zl, h):
        return shard_copy(zl * PAIR + x, h, pair_send.at[zl, h], at(z, other))

    def arrived(owner, h):
        shard_copy(owner, h, pair_send.at[0, h], at(z, other)).wait_recv()

    def inside(zz):
        return jnp.logical_and(zz >= 0, zz < line)

    load_t.wait()
    for h in range(HALVES):
        for d in (0, 1):
            @pl.when(inside(z - (2 * d - 1)))
            def _():
                line_copy(d, z, h).start()
        pair_copy(z, h).start()

    load_f.wait()
    swap = pltpu.make_async_remote_copy(
        src_ref=fv.at[:, half], dst_ref=fv.at[:, half], send_sem=mode_sem.at[0],
        recv_sem=mode_sem.at[1], device_id=(g, s, 1 - c), device_id_type=MESH,
    )
    swap.start()
    px[...] = jnp.zeros_like(px)
    pf[...] = jnp.zeros_like(pf)
    wacc[...] = jnp.zeros_like(wacc)
    load_d.wait()
    other_half = pl.ds(pl.multiple_of((1 - c) * own_modes, LANES), own_modes)

    def prepare(owner):
        d_cols = dv[:, cols(owner)]
        f_cols = fv[:, cols(owner)]
        dt[owner] = d_cols.T
        ft[owner] = f_cols.T
        product = d_cols.astype(jnp.float32) * f_cols.astype(jnp.float32)
        total = product[:, :LANES]
        for b in range(1, rows // LANES):
            total += product[:, b * LANES:(b + 1) * LANES]
        wacc[...] += total

    def project(owner):
        block = tb[owner]
        px[...] += jnp.dot(dv[:, cols(owner)], block, preferred_element_type=jnp.float32)
        pf[...] += jnp.dot(fv[:, cols(owner)], block, preferred_element_type=jnp.float32)

    def gather_step(t, carry):
        for h in range(HALVES):
            for d in (0, 1):
                sgn = 2 * d - 1
                zl = z + sgn * t

                @pl.when(inside(zl))
                def _():
                    arrived(zl * PAIR + x, h)

                    @pl.when(inside(z - sgn))
                    def _():
                        line_copy(d, zl, h).start()

                    pair_copy(zl, h).start()

            if h == 0:
                @pl.when(t == 1)
                def _():
                    pltpu.make_async_remote_copy(
                        src_ref=fv.at[:, other_half], dst_ref=fv.at[:, other_half],
                        send_sem=mode_sem.at[0], recv_sem=mode_sem.at[1],
                        device_id=(g, s, 1 - c), device_id_type=MESH,
                    ).wait_recv()

            if h < PAIR:
                @pl.when(t <= line)
                def _():
                    for k in range(h, PAIR, HALVES):
                        prepare((t - 1) * PAIR + k)

            if h == 0:
                u = t - 1
                for d in (0, 1):
                    zu = z + (2 * d - 1) * u

                    @pl.when(jnp.logical_and(inside(zu), u >= d))
                    def _():
                        project(zu * PAIR + x)

        v = t - 2
        for d in (0, 1):
            zv = z + (2 * d - 1) * v

            @pl.when(jnp.logical_and(inside(zv), v >= d))
            def _():
                for h in range(HALVES):
                    arrived(zv * PAIR + other, h)
                project(zv * PAIR + other)

        return carry

    lax.fori_loop(1, line + 2, gather_step, 0)

    weights = jnp.sum(wacc[...], axis=1, keepdims=True) / math.sqrt(modes)
    sx[...] = (weights * px[...]).astype(jnp.bfloat16)
    sf[...] = (weights * pf[...]).astype(jnp.bfloat16)

    def term(owner, h):
        return jnp.dot(dt[owner, tile(h)], sf[...], preferred_element_type=jnp.float32) + jnp.dot(
            ft[owner, tile(h)], sx[...], preferred_element_type=jnp.float32
        )

    def goal(q):
        return lax.rem(z + 1 + q // HALVES, line)

    def x_copy(q):
        return pltpu.make_async_remote_copy(
            src_ref=xsend.at[q], dst_ref=xrecv.at[q], send_sem=xs_sem.at[q],
            recv_sem=xr_sem.at[q], device_id=at(z, other), device_id_type=MESH,
        )

    def z_copy(q):
        return pltpu.make_async_remote_copy(
            src_ref=zsend.at[q], dst_ref=zrecv.at[q], send_sem=zs_sem.at[q],
            recv_sem=zr_sem.at[q], device_id=at(goal(q), x), device_id_type=MESH,
        )

    def send_pair(q, carry):
        xsend[q] = term(goal(q) * PAIR + other, q % HALVES).astype(jnp.bfloat16)
        x_copy(q).start()
        return carry

    pieces = line * HALVES
    lax.fori_loop(0, pieces, send_pair, 0)

    def send_line(q, carry):
        own_sum[...] = term(goal(q) * PAIR + x, q % HALVES)
        x_copy(q).wait_recv()

        @pl.when(q < pieces - HALVES)
        def _():
            zsend[q] = (own_sum[...] + xrecv[q].astype(jnp.float32)).astype(jnp.bfloat16)
            z_copy(q).start()

        @pl.when(q >= pieces - HALVES)
        def _():
            out_ref[tile(q % HALVES)] = own_sum[...] + xrecv[q].astype(jnp.float32)

        return carry

    lax.fori_loop(0, pieces, send_line, 0)

    swap.wait_send()

    def drain(zl, carry):
        for h in range(HALVES):
            pair_copy(zl, h).wait_send()
            for d in (0, 1):
                sgn = 2 * d - 1
                came = (zl - z) * sgn >= 0

                @pl.when(jnp.logical_and(came, inside(z - sgn)))
                def _():
                    line_copy(d, zl, h).wait_send()

            x_copy(zl * HALVES + h).wait_send()
        return carry

    lax.fori_loop(0, line, drain, 0)

    def finish(q, carry):
        z_copy(q).wait_recv()
        out_ref[tile(q % HALVES)] += zrecv[q].astype(jnp.float32)
        z_copy(q).wait_send()
        return carry

    lax.fori_loop(0, pieces - HALVES, finish, 0)
    out_ref[...] = out_ref[...] / (2.0 * math.sqrt(displace_ref.shape[0] * n))


def kernel_shards(displace, forces, trial):
    n = lax.axis_size("sample")
    line = n // PAIR
    pieces = line * HALVES
    samples, modes = displace.shape
    rows, width = trial.shape
    bf, f32 = jnp.bfloat16, jnp.float32
    dma = pltpu.SemaphoreType.DMA
    any_spec = pl.BlockSpec(memory_space=pl.ANY)
    return pl.pallas_call(
        functools.partial(kernel, n),
        out_shape=jax.ShapeDtypeStruct((rows, width), f32),
        in_specs=[any_spec] * 3,
        out_specs=pl.BlockSpec(memory_space=pltpu.VMEM),
        scratch_shapes=[
            pltpu.VMEM((samples, modes), bf),
            pltpu.VMEM((samples, modes), bf),
            pltpu.VMEM((n, rows, samples), bf),
            pltpu.VMEM((n, rows, samples), bf),
            pltpu.VMEM((n, rows, width), bf),
            pltpu.VMEM((samples, width), f32),
            pltpu.VMEM((samples, width), f32),
            pltpu.VMEM((samples, LANES), f32),
            pltpu.VMEM((samples, width), bf),
            pltpu.VMEM((samples, width), bf),
            pltpu.VMEM((pieces, rows // HALVES, width), bf),
            pltpu.VMEM((pieces, rows // HALVES, width), bf),
            pltpu.VMEM((pieces, rows // HALVES, width), bf),
            pltpu.VMEM((pieces, rows // HALVES, width), bf),
            pltpu.VMEM((rows // HALVES, width), f32),
            dma((3,)),
            dma((2,)),
            dma((n, HALVES)),
            dma((2, line, HALVES)),
            dma((line, HALVES)),
            dma((pieces,)),
            dma((pieces,)),
            dma((pieces,)),
            dma((pieces,)),
        ],
        compiler_params=pltpu.CompilerParams(
            collective_id=0, has_side_effects=True, vmem_limit_bytes=60 * 1024 * 1024
        ),
        cost_estimate=pl.CostEstimate(
            flops=8 * samples * modes * width, bytes_accessed=4 * samples * modes, transcendentals=0
        ),
    )(displace, forces, trial)


def fits(displace, forces, trial):
    n = lax.axis_size("sample")
    rows, width = trial.shape
    samples = displace.shape[0]
    aligned = all(size % LANES == 0 for size in (rows, width, samples, forces.shape[1]))
    return aligned and n % PAIR == 0 and n > PAIR and lax.axis_size("mode") == 2


def shards(displace, forces, trial):
    if fits(displace, forces, trial):
        return kernel_shards(displace, forces, trial)
    return plain_shards(displace, forces, trial)


def solution(mesh):
    return jax.shard_map(
        shards,
        mesh=mesh,
        in_specs=(
            P(("group", "sample"), None),
            P(("group", "sample"), "mode"),
            P(("group", "sample"), "mode"),
        ),
        out_specs=P(("group", "sample"), "mode"),
        check_vma=False,
    )
```

```python
import functools
import math

import jax
import jax.numpy as jnp
from jax import lax
from jax.experimental import pallas as pl
from jax.experimental.pallas import tpu as pltpu
from jax.sharding import PartitionSpec as P

MESH = pl.DeviceIdType.MESH
PAIR = 2
LANES = 128
HALVES = 2
LAG = 2


def contract_rows(columns, scaled):
    return lax.dot_general(
        columns, scaled, (((0,), (0,)), ((), ())), preferred_element_type=jnp.float32
    )


def plain_shards(displace, forces, trial):
    full_forces = lax.all_gather(forces, "mode", axis=1, tiled=True)
    modes_all = displace.shape[1]
    own_modes = forces.shape[1]
    own_disp = lax.dynamic_slice_in_dim(displace, lax.axis_index("mode") * own_modes, own_modes, 1)
    partial_value = jnp.sum(own_disp.astype(jnp.float32) * forces.astype(jnp.float32), axis=1)
    weights = lax.psum(partial_value, "mode") / math.sqrt(modes_all)
    piece = lax.all_gather(trial, "sample", axis=0, tiled=True)
    proj_x = jnp.dot(displace, piece, preferred_element_type=jnp.float32)
    proj_f = jnp.dot(full_forces, piece, preferred_element_type=jnp.float32)
    scaled_x = (weights[:, None] * proj_x).astype(jnp.bfloat16)
    scaled_f = (weights[:, None] * proj_f).astype(jnp.bfloat16)
    samples_all = displace.shape[0] * lax.axis_size("sample")
    result = lax.psum_scatter(
        contract_rows(displace, scaled_f) + contract_rows(full_forces, scaled_x),
        "sample",
        scatter_dimension=0,
        tiled=True,
    )
    return result / (2.0 * math.sqrt(samples_all))


def kernel(n, displace_ref, forces_ref, trial_ref, out_ref, dv, fv, dt, ft, tb, px, pf, wacc, sx, sf,
           xsend, xrecv, zsend, rrecv, zrecv, keep, own_sum, local_sem, mode_sem, gather_recv, line_send, pair_send,
           xs_sem, xr_sem, zs_sem, rr_sem, zr_sem):
    line = n // PAIR
    g, s, c = lax.axis_index("group"), lax.axis_index("sample"), lax.axis_index("mode")
    z, x = s // PAIR, s % PAIR
    other = 1 - x
    rows = trial_ref.shape[0]
    modes = displace_ref.shape[1]
    own_modes = forces_ref.shape[1]
    piece = rows // HALVES

    def at(zz, xx):
        return (g, zz * PAIR + xx, c)

    def cols(owner):
        return pl.ds(pl.multiple_of(owner * rows, LANES), rows)

    half = pl.ds(pl.multiple_of(c * own_modes, LANES), own_modes)
    load_t = pltpu.make_async_copy(trial_ref, tb.at[s], local_sem.at[0])
    load_f = pltpu.make_async_copy(forces_ref, fv.at[:, half], local_sem.at[1])
    load_d = pltpu.make_async_copy(displace_ref, dv, local_sem.at[2])
    load_t.start()
    load_f.start()
    load_d.start()

    barrier = pltpu.get_barrier_semaphore()
    pl.semaphore_signal(barrier, inc=1, device_id=(g, s, 1 - c), device_id_type=MESH)
    pl.semaphore_signal(barrier, inc=1, device_id=at(z, other), device_id_type=MESH)

    def greet(j, carry):
        pl.semaphore_signal(
            barrier, inc=1, device_id=at(lax.rem(z + 1 + j, line), x), device_id_type=MESH
        )
        return carry

    lax.fori_loop(0, line - 1, greet, 0)
    pl.semaphore_wait(barrier, line + 1)

    def tile(h):
        return pl.ds(pl.multiple_of(h * piece, piece), piece)

    def shard_copy(owner, h, send_sem, target):
        part = tb.at[owner, tile(h)]
        return pltpu.make_async_remote_copy(
            src_ref=part, dst_ref=part, send_sem=send_sem,
            recv_sem=gather_recv.at[owner, h], device_id=target, device_id_type=MESH,
        )

    def line_copy(d, zl, h):
        sgn = 2 * d - 1
        return shard_copy(zl * PAIR + x, h, line_send.at[d, zl, h], at(z - sgn, x))

    def pair_copy(zl, h):
        return shard_copy(zl * PAIR + x, h, pair_send.at[zl, h], at(z, other))

    def arrived(owner, h):
        shard_copy(owner, h, pair_send.at[0, h], at(z, other)).wait_recv()

    def inside(zz):
        return jnp.logical_and(zz >= 0, zz < line)

    load_t.wait()
    for h in range(HALVES):
        for d in (0, 1):
            @pl.when(inside(z - (2 * d - 1)))
            def _():
                line_copy(d, z, h).start()
        pair_copy(z, h).start()

    load_f.wait()
    swap = pltpu.make_async_remote_copy(
        src_ref=fv.at[:, half], dst_ref=fv.at[:, half], send_sem=mode_sem.at[0],
        recv_sem=mode_sem.at[1], device_id=(g, s, 1 - c), device_id_type=MESH,
    )
    swap.start()
    px[...] = jnp.zeros_like(px)
    pf[...] = jnp.zeros_like(pf)
    wacc[...] = jnp.zeros_like(wacc)
    load_d.wait()
    other_half = pl.ds(pl.multiple_of((1 - c) * own_modes, LANES), own_modes)

    def prepare(owner):
        d_cols = dv[:, cols(owner)]
        f_cols = fv[:, cols(owner)]
        dt[owner] = d_cols.T
        ft[owner] = f_cols.T
        product = d_cols.astype(jnp.float32) * f_cols.astype(jnp.float32)
        total = product[:, :LANES]
        for b in range(1, rows // LANES):
            total += product[:, b * LANES:(b + 1) * LANES]
        wacc[...] += total

    def project(owner):
        block = tb[owner]
        px[...] += jnp.dot(dv[:, cols(owner)], block, preferred_element_type=jnp.float32)
        pf[...] += jnp.dot(fv[:, cols(owner)], block, preferred_element_type=jnp.float32)

    def gather_step(t, carry):
        for h in range(HALVES):
            for d in (0, 1):
                sgn = 2 * d - 1
                zl = z + sgn * t

                @pl.when(inside(zl))
                def _():
                    arrived(zl * PAIR + x, h)

                    @pl.when(inside(z - sgn))
                    def _():
                        line_copy(d, zl, h).start()

                    pair_copy(zl, h).start()

            if h == 0:
                @pl.when(t == 1)
                def _():
                    pltpu.make_async_remote_copy(
                        src_ref=fv.at[:, other_half], dst_ref=fv.at[:, other_half],
                        send_sem=mode_sem.at[0], recv_sem=mode_sem.at[1],
                        device_id=(g, s, 1 - c), device_id_type=MESH,
                    ).wait_recv()

            if h < PAIR:
                @pl.when(t <= line)
                def _():
                    for k in range(h, PAIR, HALVES):
                        prepare((t - 1) * PAIR + k)

            if h == 0:
                u = t - 1
                for d in (0, 1):
                    zu = z + (2 * d - 1) * u

                    @pl.when(jnp.logical_and(inside(zu), u >= d))
                    def _():
                        project(zu * PAIR + x)

        v = t - 2
        for d in (0, 1):
            zv = z + (2 * d - 1) * v

            @pl.when(jnp.logical_and(inside(zv), v >= d))
            def _():
                for h in range(HALVES):
                    arrived(zv * PAIR + other, h)
                project(zv * PAIR + other)

        return carry

    lax.fori_loop(1, line + 2, gather_step, 0)

    weights = jnp.sum(wacc[...], axis=1, keepdims=True) / math.sqrt(modes)
    sx[...] = (weights * px[...]).astype(jnp.bfloat16)
    sf[...] = (weights * pf[...]).astype(jnp.bfloat16)

    def term(owner, h):
        return jnp.dot(dt[owner, tile(h)], sf[...], preferred_element_type=jnp.float32) + jnp.dot(
            ft[owner, tile(h)], sx[...], preferred_element_type=jnp.float32
        )

    b, odd = z // 2, z % 2
    mate = z + 1 - 2 * odd
    outside = line - 2

    def goal(q):
        j = q // HALVES
        last = j // outside
        return lax.rem(2 * b + 2 + j + last * (1 - 2 * (j % 2)) * (1 - odd), line)

    def nearer(q):
        return jnp.where(goal(q) > z, odd == 1, odd == 0)

    def x_copy(q):
        return pltpu.make_async_remote_copy(
            src_ref=xsend.at[q], dst_ref=xrecv.at[q], send_sem=xs_sem.at[q],
            recv_sem=xr_sem.at[q], device_id=at(z, other), device_id_type=MESH,
        )

    def z_copy(q):
        slot = b * HALVES + q % HALVES
        return pltpu.make_async_remote_copy(
            src_ref=zsend.at[q], dst_ref=zrecv.at[slot], send_sem=zs_sem.at[q],
            recv_sem=zr_sem.at[slot], device_id=at(goal(q), x), device_id_type=MESH,
        )

    def relay_copy(q):
        return pltpu.make_async_remote_copy(
            src_ref=zsend.at[q], dst_ref=rrecv.at[q], send_sem=zs_sem.at[q],
            recv_sem=rr_sem.at[q], device_id=at(mate, x), device_id_type=MESH,
        )

    def send_pair(q, carry):
        xsend[q] = term(goal(q) * PAIR + other, q % HALVES).astype(jnp.bfloat16)
        x_copy(q).start()
        return carry

    pieces = line * HALVES
    lax.fori_loop(0, pieces, send_pair, 0)

    def send_line(q, carry):
        j = q // HALVES
        own_sum[...] = term(goal(q) * PAIR + x, q % HALVES)
        x_copy(q).wait_recv()
        own_sum[...] += xrecv[q].astype(jnp.float32)

        @pl.when(jnp.logical_and(j < outside, nearer(q)))
        def _():
            keep[q] = own_sum[...]

        @pl.when(jnp.logical_and(j < outside, jnp.logical_not(nearer(q))))
        def _():
            zsend[q] = own_sum[...].astype(jnp.bfloat16)
            relay_copy(q).start()

        @pl.when(j == outside)
        def _():
            zsend[q] = own_sum[...].astype(jnp.bfloat16)
            z_copy(q).start()

        @pl.when(j == outside + 1)
        def _():
            out_ref[tile(q % HALVES)] = own_sum[...]

        r = q - LAG

        @pl.when(jnp.logical_and(r >= 0, r < outside * HALVES))
        def _():
            @pl.when(nearer(r))
            def _():
                relay_copy(r).wait_recv()
                zsend[r] = (keep[r] + rrecv[r].astype(jnp.float32)).astype(jnp.bfloat16)
                z_copy(r).start()

        return carry

    lax.fori_loop(0, pieces, send_line, 0)

    swap.wait_send()

    def drain(zl, carry):
        for h in range(HALVES):
            pair_copy(zl, h).wait_send()
            for d in (0, 1):
                sgn = 2 * d - 1
                came = (zl - z) * sgn >= 0

                @pl.when(jnp.logical_and(came, inside(z - sgn)))
                def _():
                    line_copy(d, zl, h).wait_send()

            x_copy(zl * HALVES + h).wait_send()
        return carry

    lax.fori_loop(0, line, drain, 0)

    couples = line // 2

    def finish(i, carry):
        h = i % HALVES
        slot = lax.rem(b + 1 + i // HALVES, couples) * HALVES + h
        pltpu.make_async_remote_copy(
            src_ref=zsend.at[0], dst_ref=zrecv.at[slot], send_sem=zs_sem.at[0],
            recv_sem=zr_sem.at[slot], device_id=at(mate, x), device_id_type=MESH,
        ).wait_recv()
        out_ref[tile(h)] += zrecv[slot].astype(jnp.float32)
        return carry

    lax.fori_loop(0, couples * HALVES, finish, 0)

    def drain_line(q, carry):
        z_copy(q).wait_send()
        return carry

    lax.fori_loop(0, pieces - HALVES, drain_line, 0)
    out_ref[...] = out_ref[...] / (2.0 * math.sqrt(displace_ref.shape[0] * n))


def kernel_shards(displace, forces, trial):
    n = lax.axis_size("sample")
    line = n // PAIR
    pieces = line * HALVES
    samples, modes = displace.shape
    rows, width = trial.shape
    bf, f32 = jnp.bfloat16, jnp.float32
    dma = pltpu.SemaphoreType.DMA
    any_spec = pl.BlockSpec(memory_space=pl.ANY)
    return pl.pallas_call(
        functools.partial(kernel, n),
        out_shape=jax.ShapeDtypeStruct((rows, width), f32),
        in_specs=[any_spec] * 3,
        out_specs=pl.BlockSpec(memory_space=pltpu.VMEM),
        scratch_shapes=[
            pltpu.VMEM((samples, modes), bf),
            pltpu.VMEM((samples, modes), bf),
            pltpu.VMEM((n, rows, samples), bf),
            pltpu.VMEM((n, rows, samples), bf),
            pltpu.VMEM((n, rows, width), bf),
            pltpu.VMEM((samples, width), f32),
            pltpu.VMEM((samples, width), f32),
            pltpu.VMEM((samples, LANES), f32),
            pltpu.VMEM((samples, width), bf),
            pltpu.VMEM((samples, width), bf),
            pltpu.VMEM((pieces, rows // HALVES, width), bf),
            pltpu.VMEM((pieces, rows // HALVES, width), bf),
            pltpu.VMEM((pieces, rows // HALVES, width), bf),
            pltpu.VMEM((pieces, rows // HALVES, width), bf),
            pltpu.VMEM((pieces // 2, rows // HALVES, width), bf),
            pltpu.VMEM((pieces, rows // HALVES, width), f32),
            pltpu.VMEM((rows // HALVES, width), f32),
            dma((3,)),
            dma((2,)),
            dma((n, HALVES)),
            dma((2, line, HALVES)),
            dma((line, HALVES)),
            dma((pieces,)),
            dma((pieces,)),
            dma((pieces,)),
            dma((pieces,)),
            dma((pieces,)),
        ],
        compiler_params=pltpu.CompilerParams(
            collective_id=0, has_side_effects=True, vmem_limit_bytes=52 * 1024 * 1024
        ),
        cost_estimate=pl.CostEstimate(
            flops=8 * samples * modes * width, bytes_accessed=4 * samples * modes, transcendentals=0
        ),
    )(displace, forces, trial)


def fits(displace, forces, trial):
    n = lax.axis_size("sample")
    rows, width = trial.shape
    samples = displace.shape[0]
    aligned = all(size % LANES == 0 for size in (rows, width, samples, forces.shape[1]))
    return aligned and n % (2 * PAIR) == 0 and n > 2 * PAIR and lax.axis_size("mode") == 2


def shards(displace, forces, trial):
    if fits(displace, forces, trial):
        return kernel_shards(displace, forces, trial)
    return plain_shards(displace, forces, trial)


def solution(mesh):
    return jax.shard_map(
        shards,
        mesh=mesh,
        in_specs=(
            P(("group", "sample"), None),
            P(("group", "sample"), "mode"),
            P(("group", "sample"), "mode"),
        ),
        out_specs=P(("group", "sample"), "mode"),
        check_vma=False,
    )
```

```python
import functools
import math

import jax
import jax.numpy as jnp
from jax import lax
from jax.experimental import pallas as pl
from jax.experimental.pallas import tpu as pltpu
from jax.sharding import PartitionSpec as P

MESH = pl.DeviceIdType.MESH
PAIR = 2
LANES = 128
HALVES = 2
LAG = 2


def contract_rows(columns, scaled):
    return lax.dot_general(
        columns, scaled, (((0,), (0,)), ((), ())), preferred_element_type=jnp.float32
    )


def plain_shards(displace, forces, trial):
    full_forces = lax.all_gather(forces, "mode", axis=1, tiled=True)
    modes_all = displace.shape[1]
    own_modes = forces.shape[1]
    own_disp = lax.dynamic_slice_in_dim(displace, lax.axis_index("mode") * own_modes, own_modes, 1)
    partial_value = jnp.sum(own_disp.astype(jnp.float32) * forces.astype(jnp.float32), axis=1)
    weights = lax.psum(partial_value, "mode") / math.sqrt(modes_all)
    piece = lax.all_gather(trial, "sample", axis=0, tiled=True)
    proj_x = jnp.dot(displace, piece, preferred_element_type=jnp.float32)
    proj_f = jnp.dot(full_forces, piece, preferred_element_type=jnp.float32)
    scaled_x = (weights[:, None] * proj_x).astype(jnp.bfloat16)
    scaled_f = (weights[:, None] * proj_f).astype(jnp.bfloat16)
    samples_all = displace.shape[0] * lax.axis_size("sample")
    result = lax.psum_scatter(
        contract_rows(displace, scaled_f) + contract_rows(full_forces, scaled_x),
        "sample",
        scatter_dimension=0,
        tiled=True,
    )
    return result / (2.0 * math.sqrt(samples_all))


def kernel(n, displace_ref, forces_ref, trial_ref, out_ref, dv, fv, dt, ft, tb, px, pf, wacc, sx, sf,
           xsend, xrecv, zsend, rrecv, zrecv, mrecv, keep, own_sum, local_sem, mode_sem, gather_recv, line_send, pair_send,
           xs_sem, xr_sem, zs_sem, rr_sem, zr_sem, around_sem, m_sem):
    line = n // PAIR
    g, s, c = lax.axis_index("group"), lax.axis_index("sample"), lax.axis_index("mode")
    z, x = s // PAIR, s % PAIR
    other = 1 - x
    b, odd = z // 2, z % 2
    mate = z + 1 - 2 * odd
    rows = trial_ref.shape[0]
    modes = displace_ref.shape[1]
    own_modes = forces_ref.shape[1]
    piece = rows // HALVES

    def at(zz, xx):
        return (g, zz * PAIR + xx, c)

    def cols(owner):
        return pl.ds(pl.multiple_of(owner * rows, LANES), rows)

    half = pl.ds(pl.multiple_of(c * own_modes, LANES), own_modes)
    load_t = pltpu.make_async_copy(trial_ref, tb.at[s], local_sem.at[0])
    load_f = pltpu.make_async_copy(forces_ref, fv.at[:, half], local_sem.at[1])
    load_d = pltpu.make_async_copy(displace_ref, dv, local_sem.at[2])
    load_t.start()
    load_f.start()
    load_d.start()

    barrier = pltpu.get_barrier_semaphore()
    pl.semaphore_signal(barrier, inc=1, device_id=(g, s, 1 - c), device_id_type=MESH)
    pl.semaphore_signal(barrier, inc=1, device_id=at(z, other), device_id_type=MESH)

    def greet(j, carry):
        pl.semaphore_signal(
            barrier, inc=1, device_id=at(lax.rem(z + 1 + j, line), x), device_id_type=MESH
        )
        return carry

    lax.fori_loop(0, line - 1, greet, 0)
    pl.semaphore_wait(barrier, line + 1)

    def tile(h):
        return pl.ds(pl.multiple_of(h * piece, piece), piece)

    def shard_copy(owner, h, send_sem, target):
        part = tb.at[owner, tile(h)]
        return pltpu.make_async_remote_copy(
            src_ref=part, dst_ref=part, send_sem=send_sem,
            recv_sem=gather_recv.at[owner, h], device_id=target, device_id_type=MESH,
        )

    def line_copy(d, zl, h):
        sgn = 2 * d - 1
        return shard_copy(zl * PAIR + x, h, line_send.at[d, zl, h], at(z - sgn, x))

    def pair_copy(zl, h):
        return shard_copy(zl * PAIR + x, h, pair_send.at[zl, h], at(z, other))

    def around_copy():
        return shard_copy(z * PAIR + other, HALVES - 1, around_sem.at[0], at(mate, x))

    def arrived(owner, h):
        shard_copy(owner, h, pair_send.at[0, h], at(z, other)).wait_recv()

    def inside(zz):
        return jnp.logical_and(zz >= 0, zz < line)

    load_t.wait()
    for h in range(HALVES):
        for d in (0, 1):
            @pl.when(inside(z - (2 * d - 1)))
            def _():
                line_copy(d, z, h).start()
        pair_copy(z, h).start()

    load_f.wait()
    swap = pltpu.make_async_remote_copy(
        src_ref=fv.at[:, half], dst_ref=fv.at[:, half], send_sem=mode_sem.at[0],
        recv_sem=mode_sem.at[1], device_id=(g, s, 1 - c), device_id_type=MESH,
    )
    swap.start()
    px[...] = jnp.zeros_like(px)
    pf[...] = jnp.zeros_like(pf)
    wacc[...] = jnp.zeros_like(wacc)
    load_d.wait()
    other_half = pl.ds(pl.multiple_of((1 - c) * own_modes, LANES), own_modes)

    def prepare(owner):
        d_cols = dv[:, cols(owner)]
        f_cols = fv[:, cols(owner)]
        dt[owner] = d_cols.T
        ft[owner] = f_cols.T
        product = d_cols.astype(jnp.float32) * f_cols.astype(jnp.float32)
        total = product[:, :LANES]
        for b in range(1, rows // LANES):
            total += product[:, b * LANES:(b + 1) * LANES]
        wacc[...] += total

    def project(owner):
        block = tb[owner]
        px[...] += jnp.dot(dv[:, cols(owner)], block, preferred_element_type=jnp.float32)
        pf[...] += jnp.dot(fv[:, cols(owner)], block, preferred_element_type=jnp.float32)

    def gather_step(t, carry):
        for h in range(HALVES):
            for d in (0, 1):
                sgn = 2 * d - 1
                zl = z + sgn * t

                @pl.when(inside(zl))
                def _():
                    arrived(zl * PAIR + x, h)

                    @pl.when(inside(z - sgn))
                    def _():
                        line_copy(d, zl, h).start()

                    if h < HALVES - 1:
                        pair_copy(zl, h).start()
                    else:
                        @pl.when(zl != mate)
                        def _():
                            pair_copy(zl, h).start()

            if h == 0:
                @pl.when(t == 1)
                def _():
                    arrived(z * PAIR + other, HALVES - 1)
                    around_copy().start()

            if h == 0:
                @pl.when(t == 1)
                def _():
                    pltpu.make_async_remote_copy(
                        src_ref=fv.at[:, other_half], dst_ref=fv.at[:, other_half],
                        send_sem=mode_sem.at[0], recv_sem=mode_sem.at[1],
                        device_id=(g, s, 1 - c), device_id_type=MESH,
                    ).wait_recv()

            if h < PAIR:
                @pl.when(t <= line)
                def _():
                    for k in range(h, PAIR, HALVES):
                        prepare((t - 1) * PAIR + k)

            if h == 0:
                u = t - 1
                for d in (0, 1):
                    zu = z + (2 * d - 1) * u

                    @pl.when(jnp.logical_and(inside(zu), u >= d))
                    def _():
                        project(zu * PAIR + x)

        v = t - 2
        for d in (0, 1):
            zv = z + (2 * d - 1) * v

            @pl.when(jnp.logical_and(inside(zv), v >= d))
            def _():
                for h in range(HALVES - 1):
                    arrived(zv * PAIR + other, h)

                @pl.when(v > 0)
                def _():
                    arrived(zv * PAIR + other, HALVES - 1)

                project(zv * PAIR + other)

        return carry

    lax.fori_loop(1, line + 2, gather_step, 0)

    weights = jnp.sum(wacc[...], axis=1, keepdims=True) / math.sqrt(modes)
    sx[...] = (weights * px[...]).astype(jnp.bfloat16)
    sf[...] = (weights * pf[...]).astype(jnp.bfloat16)

    def term(owner, h):
        return jnp.dot(dt[owner, tile(h)], sf[...], preferred_element_type=jnp.float32) + jnp.dot(
            ft[owner, tile(h)], sx[...], preferred_element_type=jnp.float32
        )

    outside = line - 2

    def goal(q):
        j = q // HALVES
        last = j // outside
        return lax.rem(2 * b + 2 + j + last * (1 - 2 * (j % 2)) * (1 - odd), line)

    def nearer(q):
        return jnp.where(goal(q) > z, odd == 1, odd == 0)

    def x_copy(q):
        return pltpu.make_async_remote_copy(
            src_ref=xsend.at[q], dst_ref=xrecv.at[q], send_sem=xs_sem.at[q],
            recv_sem=xr_sem.at[q], device_id=at(z, other), device_id_type=MESH,
        )

    def z_copy(q):
        slot = b * HALVES + q % HALVES
        return pltpu.make_async_remote_copy(
            src_ref=zsend.at[q], dst_ref=zrecv.at[slot], send_sem=zs_sem.at[q],
            recv_sem=zr_sem.at[slot], device_id=at(goal(q), x), device_id_type=MESH,
        )

    def relay_copy(q):
        return pltpu.make_async_remote_copy(
            src_ref=zsend.at[q], dst_ref=rrecv.at[q], send_sem=zs_sem.at[q],
            recv_sem=rr_sem.at[q], device_id=at(mate, x), device_id_type=MESH,
        )

    pieces = line * HALVES
    skipped = outside * HALVES + HALVES - 1

    def mate_copy():
        return pltpu.make_async_remote_copy(
            src_ref=xsend.at[skipped], dst_ref=mrecv, send_sem=m_sem.at[0],
            recv_sem=m_sem.at[1], device_id=at(mate, x), device_id_type=MESH,
        )

    def send_pair(q, carry):
        xsend[q] = term(goal(q) * PAIR + other, q % HALVES).astype(jnp.bfloat16)
        x_copy(q).start()
        return carry

    send_pair(0, 0)
    xsend[skipped] = term(mate * PAIR + other, HALVES - 1).astype(jnp.bfloat16)
    mate_copy().start()
    lax.fori_loop(1, skipped, send_pair, 0)
    lax.fori_loop(skipped + 1, pieces - 1, send_pair, 0)
    own_sum[...] = term(z * PAIR + other, HALVES - 1)
    mate_copy().wait_recv()
    xsend[pieces - 1] = (own_sum[...] + mrecv[...].astype(jnp.float32)).astype(jnp.bfloat16)
    x_copy(pieces - 1).start()

    def send_line(q, carry):
        j = q // HALVES
        own_sum[...] = term(goal(q) * PAIR + x, q % HALVES)

        @pl.when(q != skipped)
        def _():
            x_copy(q).wait_recv()
            own_sum[...] += xrecv[q].astype(jnp.float32)

        @pl.when(jnp.logical_and(j < outside, nearer(q)))
        def _():
            keep[q] = own_sum[...]

        @pl.when(jnp.logical_and(j < outside, jnp.logical_not(nearer(q))))
        def _():
            zsend[q] = own_sum[...].astype(jnp.bfloat16)
            relay_copy(q).start()

        @pl.when(j == outside)
        def _():
            zsend[q] = own_sum[...].astype(jnp.bfloat16)
            z_copy(q).start()

        @pl.when(j == outside + 1)
        def _():
            out_ref[tile(q % HALVES)] = own_sum[...]

        r = q - LAG

        @pl.when(jnp.logical_and(r >= 0, r < outside * HALVES))
        def _():
            @pl.when(nearer(r))
            def _():
                relay_copy(r).wait_recv()
                zsend[r] = (keep[r] + rrecv[r].astype(jnp.float32)).astype(jnp.bfloat16)
                z_copy(r).start()

        return carry

    lax.fori_loop(0, pieces, send_line, 0)

    swap.wait_send()
    around_copy().wait_send()
    mate_copy().wait_send()

    def drain(zl, carry):
        for h in range(HALVES):
            if h < HALVES - 1:
                pair_copy(zl, h).wait_send()
            else:
                @pl.when(zl != mate)
                def _():
                    pair_copy(zl, h).wait_send()

            for d in (0, 1):
                sgn = 2 * d - 1
                came = (zl - z) * sgn >= 0

                @pl.when(jnp.logical_and(came, inside(z - sgn)))
                def _():
                    line_copy(d, zl, h).wait_send()


            @pl.when(zl * HALVES + h != skipped)
            def _():
                x_copy(zl * HALVES + h).wait_send()

        return carry

    lax.fori_loop(0, line, drain, 0)

    couples = line // 2

    def finish(i, carry):
        h = i % HALVES
        slot = lax.rem(b + 1 + i // HALVES, couples) * HALVES + h
        pltpu.make_async_remote_copy(
            src_ref=zsend.at[0], dst_ref=zrecv.at[slot], send_sem=zs_sem.at[0],
            recv_sem=zr_sem.at[slot], device_id=at(mate, x), device_id_type=MESH,
        ).wait_recv()
        out_ref[tile(h)] += zrecv[slot].astype(jnp.float32)
        return carry

    lax.fori_loop(0, couples * HALVES, finish, 0)

    def drain_line(q, carry):
        z_copy(q).wait_send()
        return carry

    lax.fori_loop(0, pieces - HALVES, drain_line, 0)
    out_ref[...] = out_ref[...] / (2.0 * math.sqrt(displace_ref.shape[0] * n))


def kernel_shards(displace, forces, trial):
    n = lax.axis_size("sample")
    line = n // PAIR
    pieces = line * HALVES
    samples, modes = displace.shape
    rows, width = trial.shape
    bf, f32 = jnp.bfloat16, jnp.float32
    dma = pltpu.SemaphoreType.DMA
    any_spec = pl.BlockSpec(memory_space=pl.ANY)
    return pl.pallas_call(
        functools.partial(kernel, n),
        out_shape=jax.ShapeDtypeStruct((rows, width), f32),
        in_specs=[any_spec] * 3,
        out_specs=pl.BlockSpec(memory_space=pltpu.VMEM),
        scratch_shapes=[
            pltpu.VMEM((samples, modes), bf),
            pltpu.VMEM((samples, modes), bf),
            pltpu.VMEM((n, rows, samples), bf),
            pltpu.VMEM((n, rows, samples), bf),
            pltpu.VMEM((n, rows, width), bf),
            pltpu.VMEM((samples, width), f32),
            pltpu.VMEM((samples, width), f32),
            pltpu.VMEM((samples, LANES), f32),
            pltpu.VMEM((samples, width), bf),
            pltpu.VMEM((samples, width), bf),
            pltpu.VMEM((pieces, rows // HALVES, width), bf),
            pltpu.VMEM((pieces, rows // HALVES, width), bf),
            pltpu.VMEM((pieces, rows // HALVES, width), bf),
            pltpu.VMEM((pieces, rows // HALVES, width), bf),
            pltpu.VMEM((pieces // 2, rows // HALVES, width), bf),
            pltpu.VMEM((rows // HALVES, width), bf),
            pltpu.VMEM((pieces, rows // HALVES, width), f32),
            pltpu.VMEM((rows // HALVES, width), f32),
            dma((3,)),
            dma((2,)),
            dma((n, HALVES)),
            dma((2, line, HALVES)),
            dma((line, HALVES)),
            dma((pieces,)),
            dma((pieces,)),
            dma((pieces,)),
            dma((pieces,)),
            dma((pieces,)),
            dma((1,)),
            dma((2,)),
        ],
        compiler_params=pltpu.CompilerParams(
            collective_id=0, has_side_effects=True, vmem_limit_bytes=52 * 1024 * 1024
        ),
        cost_estimate=pl.CostEstimate(
            flops=8 * samples * modes * width, bytes_accessed=4 * samples * modes, transcendentals=0
        ),
    )(displace, forces, trial)


def fits(displace, forces, trial):
    n = lax.axis_size("sample")
    rows, width = trial.shape
    samples = displace.shape[0]
    aligned = all(size % LANES == 0 for size in (rows, width, samples, forces.shape[1]))
    return aligned and n % (2 * PAIR) == 0 and n > 2 * PAIR and lax.axis_size("mode") == 2


def shards(displace, forces, trial):
    if fits(displace, forces, trial):
        return kernel_shards(displace, forces, trial)
    return plain_shards(displace, forces, trial)


def solution(mesh):
    return jax.shard_map(
        shards,
        mesh=mesh,
        in_specs=(
            P(("group", "sample"), None),
            P(("group", "sample"), "mode"),
            P(("group", "sample"), "mode"),
        ),
        out_specs=P(("group", "sample"), "mode"),
        check_vma=False,
    )
```

```python
import functools
import math

import jax
import jax.numpy as jnp
from jax import lax
from jax.experimental import pallas as pl
from jax.experimental.pallas import tpu as pltpu
from jax.sharding import PartitionSpec as P

MESH = pl.DeviceIdType.MESH
PAIR = 2
LANES = 128
HALVES = 2
LAG = 2


def contract_rows(columns, scaled):
    return lax.dot_general(
        columns, scaled, (((0,), (0,)), ((), ())), preferred_element_type=jnp.float32
    )


def plain_shards(displace, forces, trial):
    full_forces = lax.all_gather(forces, "mode", axis=1, tiled=True)
    modes_all = displace.shape[1]
    own_modes = forces.shape[1]
    own_disp = lax.dynamic_slice_in_dim(displace, lax.axis_index("mode") * own_modes, own_modes, 1)
    partial_value = jnp.sum(own_disp.astype(jnp.float32) * forces.astype(jnp.float32), axis=1)
    weights = lax.psum(partial_value, "mode") / math.sqrt(modes_all)
    piece = lax.all_gather(trial, "sample", axis=0, tiled=True)
    proj_x = jnp.dot(displace, piece, preferred_element_type=jnp.float32)
    proj_f = jnp.dot(full_forces, piece, preferred_element_type=jnp.float32)
    scaled_x = (weights[:, None] * proj_x).astype(jnp.bfloat16)
    scaled_f = (weights[:, None] * proj_f).astype(jnp.bfloat16)
    samples_all = displace.shape[0] * lax.axis_size("sample")
    result = lax.psum_scatter(
        contract_rows(displace, scaled_f) + contract_rows(full_forces, scaled_x),
        "sample",
        scatter_dimension=0,
        tiled=True,
    )
    return result / (2.0 * math.sqrt(samples_all))


def kernel(n, displace_ref, forces_ref, trial_ref, out_ref, dv, fv, dt, ft, tb, px, pf, wacc, sx, sf,
           xsend, xrecv, zsend, rrecv, zrecv, keep, own_sum, local_sem, mode_sem, gather_recv, line_send, pair_send,
           xs_sem, xr_sem, zs_sem, rr_sem, zr_sem, around_sem):
    line = n // PAIR
    g, s, c = lax.axis_index("group"), lax.axis_index("sample"), lax.axis_index("mode")
    z, x = s // PAIR, s % PAIR
    other = 1 - x
    b, odd = z // 2, z % 2
    mate = z + 1 - 2 * odd
    rows = trial_ref.shape[0]
    modes = displace_ref.shape[1]
    own_modes = forces_ref.shape[1]
    piece = rows // HALVES

    def at(zz, xx):
        return (g, zz * PAIR + xx, c)

    def cols(owner):
        return pl.ds(pl.multiple_of(owner * rows, LANES), rows)

    half = pl.ds(pl.multiple_of(c * own_modes, LANES), own_modes)
    load_t = pltpu.make_async_copy(trial_ref, tb.at[s], local_sem.at[0])
    load_f = pltpu.make_async_copy(forces_ref, fv.at[:, half], local_sem.at[1])
    load_d = pltpu.make_async_copy(displace_ref, dv, local_sem.at[2])
    load_t.start()
    load_f.start()
    load_d.start()

    barrier = pltpu.get_barrier_semaphore()
    pl.semaphore_signal(barrier, inc=1, device_id=(g, s, 1 - c), device_id_type=MESH)
    pl.semaphore_signal(barrier, inc=1, device_id=at(z, other), device_id_type=MESH)

    def greet(j, carry):
        pl.semaphore_signal(
            barrier, inc=1, device_id=at(lax.rem(z + 1 + j, line), x), device_id_type=MESH
        )
        return carry

    lax.fori_loop(0, line - 1, greet, 0)
    pl.semaphore_wait(barrier, line + 1)

    def tile(h):
        return pl.ds(pl.multiple_of(h * piece, piece), piece)

    def shard_copy(owner, h, send_sem, target):
        part = tb.at[owner, tile(h)]
        return pltpu.make_async_remote_copy(
            src_ref=part, dst_ref=part, send_sem=send_sem,
            recv_sem=gather_recv.at[owner, h], device_id=target, device_id_type=MESH,
        )

    def line_copy(d, zl, h):
        sgn = 2 * d - 1
        return shard_copy(zl * PAIR + x, h, line_send.at[d, zl, h], at(z - sgn, x))

    def pair_copy(zl, h):
        return shard_copy(zl * PAIR + x, h, pair_send.at[zl, h], at(z, other))

    def around_copy():
        return shard_copy(z * PAIR + other, HALVES - 1, around_sem.at[0], at(mate, x))

    def arrived(owner, h):
        shard_copy(owner, h, pair_send.at[0, h], at(z, other)).wait_recv()

    def inside(zz):
        return jnp.logical_and(zz >= 0, zz < line)

    load_t.wait()
    for h in range(HALVES):
        for d in (0, 1):
            @pl.when(inside(z - (2 * d - 1)))
            def _():
                line_copy(d, z, h).start()
        pair_copy(z, h).start()

    load_f.wait()
    swap = pltpu.make_async_remote_copy(
        src_ref=fv.at[:, half], dst_ref=fv.at[:, half], send_sem=mode_sem.at[0],
        recv_sem=mode_sem.at[1], device_id=(g, s, 1 - c), device_id_type=MESH,
    )
    swap.start()
    px[...] = jnp.zeros_like(px)
    pf[...] = jnp.zeros_like(pf)
    wacc[...] = jnp.zeros_like(wacc)
    load_d.wait()
    other_half = pl.ds(pl.multiple_of((1 - c) * own_modes, LANES), own_modes)

    def prepare(owner):
        d_cols = dv[:, cols(owner)]
        f_cols = fv[:, cols(owner)]
        dt[owner] = d_cols.T
        ft[owner] = f_cols.T
        product = d_cols.astype(jnp.float32) * f_cols.astype(jnp.float32)
        total = product[:, :LANES]
        for b in range(1, rows // LANES):
            total += product[:, b * LANES:(b + 1) * LANES]
        wacc[...] += total

    def project(owner):
        block = tb[owner]
        px[...] += jnp.dot(dv[:, cols(owner)], block, preferred_element_type=jnp.float32)
        pf[...] += jnp.dot(fv[:, cols(owner)], block, preferred_element_type=jnp.float32)

    def gather_step(t, carry):
        for h in range(HALVES):
            for d in (0, 1):
                sgn = 2 * d - 1
                zl = z + sgn * t

                @pl.when(inside(zl))
                def _():
                    arrived(zl * PAIR + x, h)

                    @pl.when(inside(z - sgn))
                    def _():
                        line_copy(d, zl, h).start()

                    if h < HALVES - 1:
                        pair_copy(zl, h).start()
                    else:
                        @pl.when(zl != mate)
                        def _():
                            pair_copy(zl, h).start()

            if h == 0:
                @pl.when(t == 1)
                def _():
                    arrived(z * PAIR + other, HALVES - 1)
                    around_copy().start()

            if h == 0:
                @pl.when(t == 1)
                def _():
                    pltpu.make_async_remote_copy(
                        src_ref=fv.at[:, other_half], dst_ref=fv.at[:, other_half],
                        send_sem=mode_sem.at[0], recv_sem=mode_sem.at[1],
                        device_id=(g, s, 1 - c), device_id_type=MESH,
                    ).wait_recv()

            if h < PAIR:
                @pl.when(t <= line)
                def _():
                    for k in range(h, PAIR, HALVES):
                        prepare((t - 1) * PAIR + k)

            if h == 0:
                u = t - 1
                for d in (0, 1):
                    zu = z + (2 * d - 1) * u

                    @pl.when(jnp.logical_and(inside(zu), u >= d))
                    def _():
                        project(zu * PAIR + x)

        v = t - 2
        for d in (0, 1):
            zv = z + (2 * d - 1) * v

            @pl.when(jnp.logical_and(inside(zv), v >= d))
            def _():
                for h in range(HALVES - 1):
                    arrived(zv * PAIR + other, h)

                @pl.when(v > 0)
                def _():
                    arrived(zv * PAIR + other, HALVES - 1)

                project(zv * PAIR + other)

        return carry

    lax.fori_loop(1, line + 2, gather_step, 0)

    weights = jnp.sum(wacc[...], axis=1, keepdims=True) / math.sqrt(modes)
    sx[...] = (weights * px[...]).astype(jnp.bfloat16)
    sf[...] = (weights * pf[...]).astype(jnp.bfloat16)

    def term(owner, h):
        return jnp.dot(dt[owner, tile(h)], sf[...], preferred_element_type=jnp.float32) + jnp.dot(
            ft[owner, tile(h)], sx[...], preferred_element_type=jnp.float32
        )

    outside = line - 2

    def goal(q):
        j = q // HALVES
        last = j // outside
        return lax.rem(2 * b + 2 + j + last * (1 - 2 * (j % 2)) * (1 - odd), line)

    def nearer(q):
        return jnp.where(goal(q) > z, odd == 1, odd == 0)

    def x_copy(q):
        return pltpu.make_async_remote_copy(
            src_ref=xsend.at[q], dst_ref=xrecv.at[q], send_sem=xs_sem.at[q],
            recv_sem=xr_sem.at[q], device_id=at(z, other), device_id_type=MESH,
        )

    def z_copy(q):
        slot = b * HALVES + q % HALVES
        return pltpu.make_async_remote_copy(
            src_ref=zsend.at[q], dst_ref=zrecv.at[slot], send_sem=zs_sem.at[q],
            recv_sem=zr_sem.at[slot], device_id=at(goal(q), x), device_id_type=MESH,
        )

    def relay_copy(q):
        return pltpu.make_async_remote_copy(
            src_ref=zsend.at[q], dst_ref=rrecv.at[q], send_sem=zs_sem.at[q],
            recv_sem=rr_sem.at[q], device_id=at(mate, x), device_id_type=MESH,
        )

    def send_pair(q, carry):
        xsend[q] = term(goal(q) * PAIR + other, q % HALVES).astype(jnp.bfloat16)
        x_copy(q).start()
        return carry

    pieces = line * HALVES
    lax.fori_loop(0, pieces, send_pair, 0)

    def send_line(q, carry):
        j = q // HALVES
        own_sum[...] = term(goal(q) * PAIR + x, q % HALVES)
        x_copy(q).wait_recv()
        own_sum[...] += xrecv[q].astype(jnp.float32)

        @pl.when(jnp.logical_and(j < outside, nearer(q)))
        def _():
            keep[q] = own_sum[...]

        @pl.when(jnp.logical_and(j < outside, jnp.logical_not(nearer(q))))
        def _():
            zsend[q] = own_sum[...].astype(jnp.bfloat16)
            relay_copy(q).start()

        @pl.when(j == outside)
        def _():
            zsend[q] = own_sum[...].astype(jnp.bfloat16)
            z_copy(q).start()

        @pl.when(j == outside + 1)
        def _():
            out_ref[tile(q % HALVES)] = own_sum[...]

        r = q - LAG

        @pl.when(jnp.logical_and(r >= 0, r < outside * HALVES))
        def _():
            @pl.when(nearer(r))
            def _():
                relay_copy(r).wait_recv()
                zsend[r] = (keep[r] + rrecv[r].astype(jnp.float32)).astype(jnp.bfloat16)
                z_copy(r).start()

        return carry

    lax.fori_loop(0, pieces, send_line, 0)

    swap.wait_send()
    around_copy().wait_send()

    def drain(zl, carry):
        for h in range(HALVES):
            if h < HALVES - 1:
                pair_copy(zl, h).wait_send()
            else:
                @pl.when(zl != mate)
                def _():
                    pair_copy(zl, h).wait_send()

            for d in (0, 1):
                sgn = 2 * d - 1
                came = (zl - z) * sgn >= 0

                @pl.when(jnp.logical_and(came, inside(z - sgn)))
                def _():
                    line_copy(d, zl, h).wait_send()

            x_copy(zl * HALVES + h).wait_send()
        return carry

    lax.fori_loop(0, line, drain, 0)

    couples = line // 2

    def finish(i, carry):
        h = i % HALVES
        slot = lax.rem(b + 1 + i // HALVES, couples) * HALVES + h
        pltpu.make_async_remote_copy(
            src_ref=zsend.at[0], dst_ref=zrecv.at[slot], send_sem=zs_sem.at[0],
            recv_sem=zr_sem.at[slot], device_id=at(mate, x), device_id_type=MESH,
        ).wait_recv()
        out_ref[tile(h)] += zrecv[slot].astype(jnp.float32)
        return carry

    lax.fori_loop(0, couples * HALVES, finish, 0)

    def drain_line(q, carry):
        z_copy(q).wait_send()
        return carry

    lax.fori_loop(0, pieces - HALVES, drain_line, 0)
    out_ref[...] = out_ref[...] / (2.0 * math.sqrt(displace_ref.shape[0] * n))


def kernel_shards(displace, forces, trial):
    n = lax.axis_size("sample")
    line = n // PAIR
    pieces = line * HALVES
    samples, modes = displace.shape
    rows, width = trial.shape
    bf, f32 = jnp.bfloat16, jnp.float32
    dma = pltpu.SemaphoreType.DMA
    any_spec = pl.BlockSpec(memory_space=pl.ANY)
    return pl.pallas_call(
        functools.partial(kernel, n),
        out_shape=jax.ShapeDtypeStruct((rows, width), f32),
        in_specs=[any_spec] * 3,
        out_specs=pl.BlockSpec(memory_space=pltpu.VMEM),
        scratch_shapes=[
            pltpu.VMEM((samples, modes), bf),
            pltpu.VMEM((samples, modes), bf),
            pltpu.VMEM((n, rows, samples), bf),
            pltpu.VMEM((n, rows, samples), bf),
            pltpu.VMEM((n, rows, width), bf),
            pltpu.VMEM((samples, width), f32),
            pltpu.VMEM((samples, width), f32),
            pltpu.VMEM((samples, LANES), f32),
            pltpu.VMEM((samples, width), bf),
            pltpu.VMEM((samples, width), bf),
            pltpu.VMEM((pieces, rows // HALVES, width), bf),
            pltpu.VMEM((pieces, rows // HALVES, width), bf),
            pltpu.VMEM((pieces, rows // HALVES, width), bf),
            pltpu.VMEM((pieces, rows // HALVES, width), bf),
            pltpu.VMEM((pieces // 2, rows // HALVES, width), bf),
            pltpu.VMEM((pieces, rows // HALVES, width), f32),
            pltpu.VMEM((rows // HALVES, width), f32),
            dma((3,)),
            dma((2,)),
            dma((n, HALVES)),
            dma((2, line, HALVES)),
            dma((line, HALVES)),
            dma((pieces,)),
            dma((pieces,)),
            dma((pieces,)),
            dma((pieces,)),
            dma((pieces,)),
            dma((1,)),
        ],
        compiler_params=pltpu.CompilerParams(
            collective_id=0, has_side_effects=True, vmem_limit_bytes=52 * 1024 * 1024
        ),
        cost_estimate=pl.CostEstimate(
            flops=8 * samples * modes * width, bytes_accessed=4 * samples * modes, transcendentals=0
        ),
    )(displace, forces, trial)


def fits(displace, forces, trial):
    n = lax.axis_size("sample")
    rows, width = trial.shape
    samples = displace.shape[0]
    aligned = all(size % LANES == 0 for size in (rows, width, samples, forces.shape[1]))
    return aligned and n % (2 * PAIR) == 0 and n > 2 * PAIR and lax.axis_size("mode") == 2


def shards(displace, forces, trial):
    if fits(displace, forces, trial):
        return kernel_shards(displace, forces, trial)
    return plain_shards(displace, forces, trial)


def solution(mesh):
    return jax.shard_map(
        shards,
        mesh=mesh,
        in_specs=(
            P(("group", "sample"), None),
            P(("group", "sample"), "mode"),
            P(("group", "sample"), "mode"),
        ),
        out_specs=P(("group", "sample"), "mode"),
        check_vma=False,
    )
```
